32 devices in a mesh: ctx: 16 (over z, y, core), head: 2 (over x).
Axes of the slice: x: 2, y: 2, z: 4, core: 2. Of those that a mesh axis runs over, the one named last changes fastest.
Arguments:
- residual: bfloat16 [4096, 1024], P(('ctx', 'head')), may hold values from -6 to 6
- input_gain: float32 [2, 1024], replicated, may hold values from 0.25 to 1.75
- project_in: bfloat16 [2, 3, 1024, 1024], P(None, None, None, 'head'), may hold values from -0.1875 to 0.1875
- output_gain: float32 [2, 1024], P(None, 'head'), may hold values from 0.25 to 1.75
- project_out: bfloat16 [2, 1024, 1024], P(None, 'head'), may hold values from -0.1875 to 0.1875
Outputs:
- result_rows: bfloat16 [4096, 1024], P(('ctx', 'head'))
The draws below stay inside these ranges and needn't reach their ends.
All inputs are finite; a program needn't handle non-finite values.
Results may differ from the reference program's by a relative error of at most 0.012.
Values may be sent and summed in bfloat16 or wider, within the bound.
No kernel may reach another device: no remote copies, remote signals or barrier semaphores. Data moves between devices by JAX's collectives and lax.ppermute only.
A program may use at most 192 MiB of HBM per device.

```python
import jax
import jax.numpy as jnp
import numpy as np
from jax import lax

D = 1024
HEADS = 16
HD = 64
LAYERS = 2
CTX_TOK = 256
FEAT = 2080
TOKENS = 4096
N_CTX = 16


def shard_levels(rng, shape, pieces, least, largest):
    level, own = 1.0, jax.random.fold_in(rng, 6)
    for position, parts in pieces:
        heights = jnp.exp(jax.random.uniform(jax.random.fold_in(own, position), (parts,), jnp.float32, least / len(pieces), largest / len(pieces)))
        level = level * jnp.repeat(heights, shape[position] // parts).reshape([-1 if axis == position else 1 for axis in range(len(shape))])
    return level


def bell_draw(own_key, shape, scale, reach, shards=(), held_as=jnp.bfloat16):
    result = scale * jax.random.normal(own_key, shape, jnp.float32)
    if shards:
        result = result * shard_levels(own_key, shape, shards, -0.22, 0.18)
    return jnp.clip(result, -reach, reach).astype(held_as)


def setup_inputs(seed: int = 0) -> dict:
    key_of = jax.random.split(jax.random.key(seed), 6)
    return {
        "residual": bell_draw(key_of[0], (TOKENS, D), 1.0, 6.0, ((0, 32),)),
        "input_gain": jnp.clip(1.0 + 0.15 * jax.random.normal(key_of[1], (LAYERS, D), jnp.float32), 0.25, 1.75),
        "project_in": bell_draw(key_of[2], (LAYERS, 3, D, HEADS * HD), D ** -0.5, 0.1875, ((3, 2),)),
        "output_gain": jnp.clip(1.0 + 0.15 * jax.random.normal(key_of[3], (LAYERS, HEADS * HD), jnp.float32), 0.25, 1.75),
        "project_out": bell_draw(key_of[4], (LAYERS, HEADS * HD, D), (HEADS * HD) ** -0.5, 0.1875, ((1, 2),)),
    }


epsilon = 1e-06

def features(rows):
    width = rows.shape[-1]
    first, second = np.triu_indices(width)
    factor = jnp.asarray(np.where(first == second, 1.0, np.sqrt(2.0)), jnp.float32)
    wide = rows.astype(jnp.float32)
    return (wide[:, first] * wide[:, second] * factor).astype(jnp.bfloat16)

def rms_scale(values, gain):
    mean_square = lax.optimization_barrier(jnp.mean(values * values, axis=-1, keepdims=True))
    return values * lax.rsqrt(mean_square + epsilon) * gain

def head_block(query, key, value, prior, gain):
    count = query.shape[0]
    scores = jnp.dot(query, key.T, preferred_element_type=jnp.float32)
    places = jnp.arange(count, dtype=jnp.int32)
    causal = places[:, None] >= places[None, :]
    weights = jnp.where(causal, scores * scores, 0.0).astype(jnp.bfloat16)
    inner = jnp.dot(weights, value, preferred_element_type=jnp.float32)
    outer = jnp.dot(features(query).astype(jnp.float32), prior, precision=lax.Precision.HIGHEST)
    state = jnp.dot(features(key).T, value, preferred_element_type=jnp.float32)
    mixed = rms_scale(inner + outer, gain).astype(jnp.bfloat16)
    return (mixed, state)

def reference(residual, input_gain, project_in, output_gain, project_out):
    for layer in range(LAYERS):
        wide = residual.astype(jnp.float32)
        normed = rms_scale(wide, input_gain[layer]).astype(jnp.bfloat16)
        shaped = []
        for which in range(3):
            field = jnp.dot(normed, project_in[layer, which], preferred_element_type=jnp.float32).astype(jnp.bfloat16)
            shaped.append(field.reshape(N_CTX, CTX_TOK, HEADS, HD).transpose(0, 2, 1, 3))
        gains = output_gain[layer].reshape(HEADS, HD)

        def shard_step(prior, inputs):
            query, key, value = inputs
            mixed, state = jax.vmap(head_block)(query, key, value, prior, gains)
            return (prior + state, mixed)
        initial = jnp.zeros((HEADS, FEAT, HD), jnp.float32)
        ending, mixed = lax.scan(shard_step, initial, (shaped[0], shaped[1], shaped[2]))
        merged = mixed.transpose(0, 2, 1, 3).reshape(TOKENS, HEADS * HD)
        delta = jnp.dot(merged, project_out[layer], preferred_element_type=jnp.float32)
        residual = (wide + delta).astype(jnp.bfloat16)
    return residual
```

```python
import functools

import jax
import jax.numpy as jnp
from jax import lax
from jax.experimental import pallas as pl
from jax.experimental.pallas import tpu as pltpu
from jax.sharding import PartitionSpec as P

HD = 64
LAYERS = 2
EPSILON = 1e-06


def rms_scale(values, gain):
    mean_square = jnp.mean(values * values, axis=-1, keepdims=True)
    return values * lax.rsqrt(mean_square + EPSILON) * gain


def project_kernel(place, row_refs, gain_ref, weight_ref, out_ref, normed):
    rows = row_refs[0].shape[0]

    @pl.when(pl.program_id(0) == 0)
    def _():
        gain = gain_ref[...]
        for which, ref in enumerate(row_refs):
            scaled = rms_scale(ref[...].astype(jnp.float32), gain).astype(jnp.bfloat16)
            if len(row_refs) == 1:
                normed[...] = scaled
            else:
                start = place() if which == 0 else 1 - place()
                normed[pl.ds(pl.multiple_of(start * rows, rows), rows), :] = scaled

    field = jnp.dot(normed[...], weight_ref[...], preferred_element_type=jnp.float32)
    flipped = field.T.astype(jnp.bfloat16)
    for head in range(out_ref.shape[0]):
        out_ref[head] = flipped[head * HD : (head + 1) * HD]


def project(layer, rows, gain, project_in, place):
    width, columns = project_in.shape[2:]
    tokens = sum(r.shape[0] for r in rows)
    heads = columns // HD

    def kernel(*refs):
        project_kernel(place, refs[: len(rows)], *refs[len(rows) :])

    return pl.pallas_call(
        kernel,
        grid=(3,),
        in_specs=[pl.BlockSpec(r.shape, lambda m: (0, 0)) for r in rows]
        + [
            pl.BlockSpec((None, 1, width), lambda m: (layer, 0, 0)),
            pl.BlockSpec((None, None, width, columns), lambda m: (layer, m, 0, 0)),
        ],
        out_specs=pl.BlockSpec((heads, HD, tokens), lambda m: (0, m, 0)),
        out_shape=jax.ShapeDtypeStruct((heads, 3 * HD, tokens), jnp.bfloat16),
        scratch_shapes=[pltpu.VMEM((tokens, width), jnp.bfloat16)],
        compiler_params=pltpu.CompilerParams(vmem_limit_bytes=32 * 2**20),
        cost_estimate=pl.CostEstimate(
            flops=6 * tokens * width * columns, bytes_accessed=6 * width * columns, transcendentals=0
        ),
    )(*rows, gain, project_in)


def attention_kernel(shift_ref, own_ref, others_ref, gain_ref, out_ref, values):
    groups, _, tokens = own_ref.shape
    split = out_ref.shape[0]
    own_slot = others_ref.shape[0] if others_ref.shape[0] == 1 else None
    sources = others_ref.shape[0] + (own_slot is not None)

    def block(source, group, part):
        if source == own_slot:
            return own_ref[group, (1 + part) * HD : (2 + part) * HD, :]
        return others_ref[source, group, part * HD : (part + 1) * HD, :]

    for group in range(groups):
        for source in range(sources):
            values[group, source * tokens : (source + 1) * tokens, :] = block(source, group, 1).T
    offset = lax.broadcasted_iota(jnp.int32, (tokens, tokens), 1) - lax.broadcasted_iota(
        jnp.int32, (tokens, tokens), 0
    )
    gain = gain_ref[...]
    for group in range(groups):
        query = own_ref[group, :HD, :].T
        total = jnp.zeros((tokens, HD), jnp.float32)
        for past in range(group + 1):
            for source in range(sources):
                scores = jnp.dot(query, block(source, past, 0), preferred_element_type=jnp.float32)
                weights = scores * scores
                if past == group:
                    weights = jnp.where(offset <= shift_ref[source], weights, 0.0)
                total += jnp.dot(
                    weights.astype(jnp.bfloat16),
                    values[past, source * tokens : (source + 1) * tokens, :],
                    preferred_element_type=jnp.float32,
                )
        flipped = rms_scale(total, gain).T.astype(jnp.bfloat16)
        part = tokens // split
        for piece in range(split):
            out_ref[piece, group] = flipped[:, piece * part : (piece + 1) * part]


def attention(shift, own, others, gain, split):
    groups, _, tokens = own.shape
    sources = shift.shape[0]
    pairs = groups * (groups + 1) // 2 * sources * tokens * tokens
    return pl.pallas_call(
        attention_kernel,
        in_specs=[pl.BlockSpec(memory_space=pltpu.SMEM)] + [pl.BlockSpec(memory_space=pltpu.VMEM)] * 3,
        out_specs=pl.BlockSpec(memory_space=pltpu.VMEM),
        out_shape=jax.ShapeDtypeStruct((split, groups, HD, tokens // split), jnp.bfloat16),
        scratch_shapes=[pltpu.VMEM((groups, sources * tokens, HD), jnp.bfloat16)],
        compiler_params=pltpu.CompilerParams(vmem_limit_bytes=48 * 2**20),
        cost_estimate=pl.CostEstimate(flops=4 * pairs * HD, bytes_accessed=2**21, transcendentals=0),
    )(shift, own, others, gain)


def mix_kernel(place, mixed_ref, residual_ref, weight_refs, out_ref):
    depth = weight_refs[0].shape[0]
    total = residual_ref[...].astype(jnp.float32)
    for which, ref in enumerate(weight_refs):
        if len(weight_refs) == 1:
            mixed = mixed_ref[...]
        else:
            start = place() if which == 0 else 1 - place()
            mixed = mixed_ref[pl.ds(pl.multiple_of(start * depth, depth), depth), :]
        total += jnp.dot(mixed.T, ref[...], preferred_element_type=jnp.float32)
    out_ref[...] = total.astype(jnp.bfloat16)


def mix(mixed, residual, weights, place):
    depth, rows = mixed.shape
    width = residual.shape[1]
    steps = 4 if width % 1024 == 0 else 1

    def kernel(mixed_ref, residual_ref, *refs):
        mix_kernel(place, mixed_ref, residual_ref, refs[:-1], refs[-1])

    return pl.pallas_call(
        kernel,
        grid=(steps,),
        in_specs=[
            pl.BlockSpec((depth, rows), lambda n: (0, 0)),
            pl.BlockSpec((rows, width // steps), lambda n: (0, n)),
        ]
        + [pl.BlockSpec((w.shape[0], width // steps), lambda n: (0, n)) for w in weights],
        out_specs=pl.BlockSpec((rows, width // steps), lambda n: (0, n)),
        out_shape=jax.ShapeDtypeStruct(residual.shape, jnp.bfloat16),
        compiler_params=pltpu.CompilerParams(vmem_limit_bytes=32 * 2**20),
        cost_estimate=pl.CostEstimate(
            flops=2 * rows * width * depth, bytes_accessed=2 * width * depth, transcendentals=0
        ),
    )(mixed, residual, *weights)


def per_device(residual, input_gain, project_in, output_gain, project_out):
    shards, split = lax.axis_size("ctx"), lax.axis_size("head")
    local_heads = output_gain.shape[1] // HD
    replicas = shards // local_heads
    index = lax.axis_index("ctx")
    replica = index % replicas
    paired = split == 2
    swap = [(0, 1), (1, 0)]

    def place():
        return lax.axis_index("head")

    shard_groups = [[k * replicas + r for k in range(local_heads)] for r in range(replicas)]
    row_groups = [[c * split + x for x in range(split) for c in group] for group in shard_groups]
    head_groups = [[k * replicas + r for r in range(replicas)] for k in range(local_heads)]

    def other_half(weights):
        depth = weights.shape[0]
        near = index % 2
        half = lax.dynamic_slice_in_dim(weights, near * (depth // 2), depth // 2, axis=0)
        mine = lax.ppermute(half, "head", swap)
        theirs = lax.ppermute(mine, "ctx", [(c, c ^ 1) for c in range(shards)])
        return lax.cond(
            near == 0,
            lambda: jnp.concatenate([mine, theirs], axis=0),
            lambda: jnp.concatenate([theirs, mine], axis=0),
        )

    gains_in = input_gain[:, None, :]
    for layer in range(LAYERS):
        if paired:
            rows = [residual, lax.ppermute(residual, "head", swap)]
            held, _ = lax.optimization_barrier((project_out[layer], rows[1]))
            weights_out = [project_out[layer], other_half(held)]
        else:
            rows = [lax.all_gather(residual, "head", axis=0, tiled=True)]
            weights_out = [lax.all_gather(project_out[layer], "head", axis=0, tiled=True)]
        fields = project(layer, rows, gains_in, project_in, place)
        own = lax.all_to_all(fields, "ctx", 0, 0, axis_index_groups=shard_groups, tiled=True)
        tokens = own.shape[2]
        if replicas == 2:
            others = lax.ppermute(own[None, :, HD:], "ctx", [(c, c ^ 1) for c in range(shards)])
            shift = jnp.stack([2 * replica - 1, 0 * replica]) * tokens
        else:
            others = lax.all_gather(own[:, HD:], "ctx", axis=0, axis_index_groups=head_groups)
            shift = (replica - jnp.arange(replicas)) * tokens
        gain = lax.dynamic_slice_in_dim(output_gain[layer], index // replicas * HD, HD)[None]
        heads = attention(shift.astype(jnp.int32), own, others, gain, split)
        heads = heads.reshape(split * local_heads, HD, tokens // split)
        mixed = lax.all_to_all(heads, ("ctx", "head"), 0, 0, axis_index_groups=row_groups, tiled=True)
        mixed = mixed.reshape(split * local_heads * HD, tokens // split)
        residual = mix(mixed, residual, weights_out, place)
    return residual


def solution(mesh):
    return jax.shard_map(
        per_device,
        mesh=mesh,
        in_specs=(
            P(("ctx", "head"), None),
            P(),
            P(None, None, None, "head"),
            P(None, "head"),
            P(None, "head", None),
        ),
        out_specs=P(("ctx", "head"), None),
        check_vma=False,
    )
```

```python
import functools

import jax
import jax.numpy as jnp
from jax import lax
from jax.experimental import pallas as pl
from jax.experimental.pallas import tpu as pltpu
from jax.sharding import PartitionSpec as P

HD = 64
LAYERS = 2
EPSILON = 1e-06
GRANT = 16 * 2**20
VMEM = pl.BlockSpec(memory_space=pltpu.VMEM)


def rms_scale(values, gain):
    mean_square = jnp.mean(values * values, axis=-1, keepdims=True)
    return values * lax.rsqrt(mean_square + EPSILON) * gain


def project_kernel(layer, row_ref, gain_ref, weight_ref, out_ref, normed):
    @pl.when(pl.program_id(0) == 0)
    def _():
        gain = gain_ref[layer : layer + 1, :]
        normed[...] = rms_scale(row_ref[...].astype(jnp.float32), gain).astype(jnp.bfloat16)

    field = jnp.dot(normed[...], weight_ref[...], preferred_element_type=jnp.float32)
    flipped = field.T.astype(jnp.bfloat16)
    for head in range(out_ref.shape[0]):
        out_ref[head] = flipped[head * HD : (head + 1) * HD]


def project(layer, rows, gain, project_in, weight=1):
    width, columns = project_in.shape[1:]
    tokens = rows.shape[0]
    heads = columns // HD
    return pl.pallas_call(
        functools.partial(project_kernel, layer),
        grid=(3,),
        in_specs=[
            pl.BlockSpec(rows.shape, lambda m: (0, 0)),
            pl.BlockSpec(gain.shape, lambda m: (0, 0)),
            pl.BlockSpec((None, width, columns), lambda m: (m, 0, 0)),
        ],
        out_specs=pl.BlockSpec((heads, HD, tokens), lambda m: (0, m, 0)),
        out_shape=jax.ShapeDtypeStruct((heads, 3 * HD, tokens), jnp.bfloat16),
        scratch_shapes=[pltpu.VMEM((tokens, width), jnp.bfloat16)],
        compiler_params=pltpu.CompilerParams(vmem_limit_bytes=GRANT),
        cost_estimate=pl.CostEstimate(
            flops=6 * tokens * width * columns * weight, bytes_accessed=6 * width * columns, transcendentals=0
        ),
    )(rows, gain, project_in)


def attention_kernel(layer, own_count, start, place, gain_ref, *refs):
    out_ref, keys, values = refs[-3:]
    own, others = refs[:own_count], refs[own_count:-3]
    sources, groups, _, tokens = keys.shape
    width = own[0].shape[-1]
    split, piece = out_ref.shape[0], out_ref.shape[-1]

    def part(source, chunk, group, which):
        rows = slice(which * HD, (which + 1) * HD)
        if sources > 2:
            return others[0][source, group, rows, :]
        return (others if source else own)[chunk][group, rows, :]

    for group in range(groups):
        for source in range(sources):
            for chunk in range(own_count):
                lanes = slice(chunk * width, (chunk + 1) * width)
                keys[source, group, :, lanes] = part(source, chunk, group, 1)
                values[source, group, lanes, :] = part(source, chunk, group, 2).T

    def shift(source):
        if sources == 2:
            return source * (2 * replica - 1)
        return replica - source

    def places(axis):
        place = lax.broadcasted_iota(jnp.int32, (tokens, tokens), axis) + start()
        return jnp.where(place >= tokens, place - tokens, place)

    ahead = places(1) - places(0)
    head, replica = place()
    gains = gain_ref[layer : layer + 1, :]
    gain = sum(
        jnp.where(head == index, gains[:, index * HD : (index + 1) * HD], 0.0) for index in range(gains.shape[1] // HD)
    )
    for group in range(groups):
        query = jnp.concatenate([ref[group, :HD, :] for ref in own], axis=1).T
        total = jnp.zeros((tokens, HD), jnp.float32)
        for past in range(group + 1):
            for source in range(sources):
                scores = jnp.dot(query, keys[source, past], preferred_element_type=jnp.float32)
                weights = scores * scores
                if past == group:
                    weights = jnp.where(ahead <= shift(source) * tokens, weights, 0.0)
                total += jnp.dot(
                    weights.astype(jnp.bfloat16), values[source, past], preferred_element_type=jnp.float32
                )
        flipped = rms_scale(total, gain).T.astype(jnp.bfloat16)
        for index in range(split):
            lanes = flipped[:, index * piece : (index + 1) * piece]
            if own_count == 1:
                out_ref[index, group] = lanes
            else:
                out_ref[start() // width if index == 0 else 1 - start() // width, group] = lanes


def attention(layer, sources, gain, own, others, start, place, split):
    groups = own[0].shape[0]
    tokens = sum(chunk.shape[2] for chunk in own)
    pairs = groups * (groups + 1) // 2 * sources * tokens * tokens

    def kernel(*refs):
        attention_kernel(layer, len(own), start, place, *refs)

    return pl.pallas_call(
        kernel,
        in_specs=[VMEM] * (1 + len(own) + len(others)),
        out_specs=VMEM,
        out_shape=jax.ShapeDtypeStruct((split, groups, HD, tokens // split), jnp.bfloat16),
        scratch_shapes=[
            pltpu.VMEM((sources, groups, HD, tokens), jnp.bfloat16),
            pltpu.VMEM((sources, groups, tokens, HD), jnp.bfloat16),
        ],
        compiler_params=pltpu.CompilerParams(vmem_limit_bytes=GRANT),
        cost_estimate=pl.CostEstimate(flops=4 * pairs * HD, bytes_accessed=2**21, transcendentals=0),
    )(gain, *own, *others)


def mix_kernel(starts, mixed_ref, residual_ref, *refs):
    weight_refs, out_ref, flipped = refs[:-2], refs[-2], refs[-1]

    @pl.when(pl.program_id(0) == 0)
    def _():
        first = 0
        for start, ref in zip(starts(), weight_refs):
            rows = ref.shape[0]
            at = start if isinstance(start, int) else pl.multiple_of(start, rows)
            flipped[:, first : first + rows] = mixed_ref[pl.ds(at, rows), :].T
            first += rows

    total, first = residual_ref[...].astype(jnp.float32), 0
    for ref in weight_refs:
        rows = ref.shape[0]
        total += jnp.dot(flipped[:, first : first + rows], ref[...], preferred_element_type=jnp.float32)
        first += rows
    out_ref[...] = total.astype(jnp.bfloat16)


def mix(mixed, residual, weights, starts):
    depth, rows = mixed.shape
    width = residual.shape[1]
    steps = 4 if width % 1024 == 0 else 1

    def kernel(*refs):
        mix_kernel(starts, *refs)

    return pl.pallas_call(
        kernel,
        grid=(steps,),
        in_specs=[
            pl.BlockSpec((depth, rows), lambda n: (0, 0)),
            pl.BlockSpec((rows, width // steps), lambda n: (0, n)),
        ]
        + [pl.BlockSpec((w.shape[0], width // steps), lambda n: (0, n)) for w in weights],
        out_specs=pl.BlockSpec((rows, width // steps), lambda n: (0, n)),
        out_shape=jax.ShapeDtypeStruct(residual.shape, jnp.bfloat16),
        scratch_shapes=[pltpu.VMEM((rows, depth), jnp.bfloat16)],
        compiler_params=pltpu.CompilerParams(vmem_limit_bytes=GRANT),
        cost_estimate=pl.CostEstimate(
            flops=2 * rows * width * depth, bytes_accessed=2 * width * depth, transcendentals=0
        ),
    )(mixed, residual, *weights)


def per_device(residual, input_gain, project_in, output_gain, project_out):
    shards, split = lax.axis_size("ctx"), lax.axis_size("head")
    depth = output_gain.shape[1]
    local_heads = depth // HD
    replicas = shards // local_heads
    paired = split == 2
    swap = [(0, 1), (1, 0)]
    neighbours = [(c, c ^ 1) for c in range(shards)]
    rows = residual.shape[0]

    shard_groups = [[k * replicas + r for k in range(local_heads)] for r in range(replicas)]
    row_groups = [[c * split + x for x in range(split) for c in group] for group in shard_groups]
    head_groups = [[k * replicas + r for r in range(replicas)] for k in range(local_heads)]

    def weight_starts():
        if not paired:
            return [0]
        mine = lax.axis_index("head")
        return [mine * depth, (1 - mine) * depth]

    def place():
        index = lax.axis_index("ctx")
        return index // replicas, index % replicas

    def first_place():
        return lax.axis_index("head") * rows if paired else 0

    before = None
    for layer in range(LAYERS):
        out, into = project_out[layer], project_in[layer]
        if paired:
            peer = lax.ppermute(residual, "head", swap)
            if before is None:
                out, _ = lax.optimization_barrier((out, peer))
            else:
                out, into, _ = lax.optimization_barrier((project_out, project_in, before))
                out, into = out[layer], into[layer]
            weights_out = [out, lax.ppermute(out, "head", swap)]
            chunks = [residual, peer]
        else:
            weights_out = [lax.all_gather(out, "head", axis=0, tiled=True)]
            chunks = [lax.all_gather(residual, "head", axis=0, tiled=True)]
        own = [
            lax.all_to_all(
                project(layer, chunk, input_gain, into, 1 + 20 * number),
                "ctx",
                0,
                0,
                axis_index_groups=shard_groups,
                tiled=True,
            )
            for number, chunk in enumerate(chunks)
        ]
        before = own[-1]
        tokens = rows * split
        if replicas == 1:
            others = []
        elif replicas == 2:
            others = [lax.ppermute(chunk, "ctx", neighbours) for chunk in own]
        else:
            own = [jnp.concatenate(own, axis=2)]
            others = [lax.all_gather(own[0], "ctx", axis=0, axis_index_groups=head_groups)]
        heads = attention(layer, replicas, output_gain, own, others, first_place, place, split)
        heads = heads.reshape(split * local_heads, HD, tokens // split)
        mixed = lax.all_to_all(heads, ("ctx", "head"), 0, 0, axis_index_groups=row_groups, tiled=True)
        mixed = mixed.reshape(split * local_heads * HD, tokens // split)
        residual = mix(mixed, residual, weights_out, weight_starts)
    return residual


def solution(mesh):
    return jax.shard_map(
        per_device,
        mesh=mesh,
        in_specs=(
            P(("ctx", "head"), None),
            P(),
            P(None, None, None, "head"),
            P(None, "head"),
            P(None, "head", None),
        ),
        out_specs=P(("ctx", "head"), None),
        check_vma=False,
    )
```

```python
import functools

import jax
import jax.numpy as jnp
from jax import lax
from jax.experimental import pallas as pl
from jax.experimental.pallas import tpu as pltpu
from jax.sharding import PartitionSpec as P

HD = 64
LAYERS = 2
EPSILON = 1e-06
VMEM = pl.BlockSpec(memory_space=pltpu.VMEM)
HBM = pl.BlockSpec(memory_space=pltpu.HBM)


def params(mebibytes):
    return pltpu.CompilerParams(vmem_limit_bytes=mebibytes * 2**20)


def rms_scale(values, gain):
    mean_square = jnp.mean(values * values, axis=-1, keepdims=True)
    return values * lax.rsqrt(mean_square + EPSILON) * gain


def fetch(pairs, semaphores):
    copies = [pltpu.make_async_copy(*pair, semaphores.at[index]) for index, pair in enumerate(pairs)]
    for copy in copies:
        copy.start()
    return copies


def project_rows(rows, gain, weights, flat, place, outs):
    normed = rms_scale(rows, gain).astype(jnp.bfloat16)
    for which in range(3):
        field = jnp.dot(normed, weights(which), preferred_element_type=jnp.float32)
        flipped = field.T.astype(jnp.bfloat16)
        part = slice(which * HD, (which + 1) * HD)
        if len(outs) == 1:
            for head in range(outs[0].shape[0]):
                outs[0][head, part, :] = flipped[head * HD : (head + 1) * HD]
        else:
            flat[...] = flipped
            for slot, out in enumerate(outs):
                start = (place()[0] ^ slot) * HD
                out[part, :] = flat[pl.ds(pl.multiple_of(start, HD), HD), :]


def project(rows, gain, weights, layer, place):
    width, columns = weights.shape[1:]
    tokens = rows.shape[0]

    def kernel(row_ref, gain_ref, weight_ref, out_ref):
        values = row_ref[...].astype(jnp.float32)
        project_rows(values, gain_ref[layer : layer + 1, :], lambda which: weight_ref[which], None, place, [out_ref])

    return pl.pallas_call(
        kernel,
        in_specs=[VMEM] * 3,
        out_specs=VMEM,
        out_shape=jax.ShapeDtypeStruct((columns // HD, 3 * HD, tokens), jnp.bfloat16),
        compiler_params=params(16),
        cost_estimate=pl.CostEstimate(
            flops=6 * tokens * width * columns, bytes_accessed=6 * width * columns, transcendentals=0
        ),
    )(rows, gain, weights)


def mix_rows(starts, mixed, residual, weights):
    total = residual.astype(jnp.float32)
    for start, weight in zip(starts, weights):
        rows = weight.shape[0]
        at = start if isinstance(start, int) else pl.multiple_of(start, rows)
        total += jnp.dot(mixed[pl.ds(at, rows), :].T, weight[...], preferred_element_type=jnp.float32)
    return total.astype(jnp.bfloat16)


def rows_step(residual, mixed=(), onward=(), place=None, slots=False, weight=1):
    rows, width = residual.shape
    operands, views, shapes, outs = [residual], [None], [(residual.shape, jnp.bfloat16)], []
    flops, itself = 0, False
    if mixed:
        entries, index, parts, starts = mixed
        operands += [entries] + list(parts)
        views += [None] + [index if len(part.shape) == 3 else None for part in parts]
        shapes += [(entries.shape, jnp.bfloat16)] + [(part.shape[-2:], jnp.bfloat16) for part in parts]
        outs.append(jax.ShapeDtypeStruct(residual.shape, jnp.bfloat16))
        flops += 2 * rows * width * entries.shape[0]
    if onward:
        layer, gain, project_in = onward
        columns = project_in.shape[-1]
        itself = len(project_in.shape) == 4
        operands += [gain] + [project_in] * (3 if itself else 1)
        views += [None] + [(layer, which) for which in range(3)]
        shapes += [(gain.shape, jnp.float32)] + [(project_in.shape[2:], jnp.bfloat16)] * 3
        shape, heads = (3 * HD, rows), columns // HD
        outs += [jax.ShapeDtypeStruct(shape if slots else (heads, *shape), jnp.bfloat16)] * (heads if slots else 1)
        flops += 6 * rows * width * columns
    count = len(operands)
    scratch = [pltpu.VMEM(*shape) for shape in shapes] + [pltpu.SemaphoreType.DMA((count,))] if itself else []
    if onward and slots:
        scratch.append(pltpu.VMEM((columns, rows), jnp.bfloat16))

    def kernel(*refs):
        sources, results, held = refs[:count], list(refs[count : count + len(outs)]), refs[count + len(outs) :]
        flat = refs[-1] if slots else None
        if itself:
            pairs = [(ref if view is None else ref.at[view], to) for ref, view, to in zip(sources, views, held)]
            copies = fetch(pairs, held[count])
        else:
            held = sources

        def arrived(index):
            if itself:
                copies[index].wait()
            return held[index]

        current, used = arrived(0)[...], 1
        if mixed:
            used = 2 + len(parts)
            current = mix_rows(starts(), arrived(1), current, [arrived(index) for index in range(2, used)])
            results.pop(0)[...] = current
        if onward:
            scale = arrived(used)[layer : layer + 1, :]

            def weights(which):
                return arrived(used + 1 + which)[...] if itself else held[used + 1][which]

            project_rows(current.astype(jnp.float32), scale, weights, flat, place, results)

    return pl.pallas_call(
        kernel,
        in_specs=[HBM if itself else VMEM] * count,
        out_specs=[VMEM] * len(outs),
        out_shape=outs,
        scratch_shapes=scratch,
        compiler_params=params(59 if itself else 16),
        cost_estimate=pl.CostEstimate(flops=flops * weight, bytes_accessed=flops // rows, transcendentals=0),
    )(*operands)


def assemble(slots, place):
    def kernel(*refs):
        for slot, ref in enumerate(refs[:-1]):
            refs[-1][place()[0] ^ slot] = ref[...]

    return pl.pallas_call(
        kernel,
        in_specs=[VMEM] * len(slots),
        out_specs=VMEM,
        out_shape=jax.ShapeDtypeStruct((len(slots), *slots[0].shape), slots[0].dtype),
        compiler_params=params(8),
        cost_estimate=pl.CostEstimate(flops=0, bytes_accessed=4 * len(slots) * slots[0].size, transcendentals=0),
    )(*slots)


def attention_kernel(layer, own_count, start, place, gain_ref, *refs):
    out_ref, keys, values = refs[-3:]
    own, others = refs[:own_count], refs[own_count:-3]
    groups, split, piece = out_ref.shape[1], out_ref.shape[0], out_ref.shape[-1]
    tokens = split * piece
    span = values.shape[1] // groups
    sources = span // tokens
    width = own[0].shape[-1]
    head, replica = place()

    def part(source, chunk, group, which):
        rows = slice(which * HD, (which + 1) * HD)
        if sources > 2:
            return others[0][source, group, rows, :]
        return (others if source else own)[chunk][group, rows, :]

    for group in range(groups):
        for source in range(sources):
            for chunk in range(own_count):
                first = group * span + source * tokens + chunk * width
                keys[first : first + width, :] = part(source, chunk, group, 1).T
                values[:, first : first + width] = part(source, chunk, group, 2)

    def shift(source):
        if sources == 2:
            return source * (2 * replica - 1)
        return replica - source

    def places(axis):
        place = lax.broadcasted_iota(jnp.int32, (tokens, tokens), axis) + start()
        return jnp.where(place >= tokens, place - tokens, place)

    ahead = places(0) - places(1)
    visible = [ahead <= shift(source) * tokens for source in range(sources)]
    gains = gain_ref[layer : layer + 1, :]
    gain = sum(
        jnp.where(head == index, gains[:, index * HD : (index + 1) * HD], 0.0) for index in range(gains.shape[1] // HD)
    ).T
    step = min(span, 512)
    for group in range(groups):
        query = jnp.concatenate([ref[group, :HD, :] for ref in own], axis=1)
        total = jnp.zeros((HD, tokens), jnp.float32)
        for first in range(0, (group + 1) * span, step):
            scores = jnp.dot(keys[first : first + step, :], query, preferred_element_type=jnp.float32)
            weights = scores * scores
            if first >= group * span:
                source = (first - group * span) // tokens
                mask = jnp.concatenate(visible[source : source + step // tokens], axis=0)
                weights = jnp.where(mask, weights, 0.0)
            total += jnp.dot(
                values[:, first : first + step], weights.astype(jnp.bfloat16), preferred_element_type=jnp.float32
            )
        mean_square = jnp.mean(total * total, axis=0, keepdims=True)
        scaled = (total * lax.rsqrt(mean_square + EPSILON) * gain).astype(jnp.bfloat16)
        for index in range(split):
            lanes = scaled[:, index * piece : (index + 1) * piece]
            if own_count == 1:
                out_ref[index, group] = lanes
            else:
                out_ref[start() // width if index == 0 else 1 - start() // width, group] = lanes


def attention(layer, sources, gain, own, others, start, place, split):
    groups = own[0].shape[0]
    tokens = sum(chunk.shape[2] for chunk in own)
    pairs = groups * (groups + 1) // 2 * sources * tokens * tokens

    def kernel(*refs):
        attention_kernel(layer, len(own), start, place, *refs)

    return pl.pallas_call(
        kernel,
        in_specs=[VMEM] * (1 + len(own) + len(others)),
        out_specs=VMEM,
        out_shape=jax.ShapeDtypeStruct((split, groups, HD, tokens // split), jnp.bfloat16),
        scratch_shapes=[
            pltpu.VMEM((groups * sources * tokens, HD), jnp.bfloat16),
            pltpu.VMEM((HD, groups * sources * tokens), jnp.bfloat16),
        ],
        compiler_params=params(16),
        cost_estimate=pl.CostEstimate(flops=4 * pairs * HD, bytes_accessed=2**21, transcendentals=0),
    )(gain, *own, *others)


def per_device(residual, input_gain, project_in, output_gain, project_out):
    shards, split = lax.axis_size("ctx"), lax.axis_size("head")
    depth = output_gain.shape[1]
    local_heads = depth // HD
    replicas = shards // local_heads
    paired = split == 2 and replicas == 2 and local_heads & (local_heads - 1) == 0
    swap = [(0, 1), (1, 0)]
    neighbours = [(c, c ^ 1) for c in range(shards)]
    rows = residual.shape[0]
    tokens = rows * split

    shard_groups = [[k * replicas + r for k in range(local_heads)] for r in range(replicas)]
    row_groups = [[c * split + x for x in range(split) for c in group] for group in shard_groups]
    head_groups = [[k * replicas + r for r in range(replicas)] for k in range(local_heads)]

    def weight_starts():
        if not paired:
            return [0]
        mine = lax.axis_index("head")
        return [mine * depth, (1 - mine) * depth]

    def place():
        index = lax.axis_index("ctx")
        return index // replicas, index % replicas

    def first_place():
        return lax.axis_index("head") * rows if paired else 0

    def to_heads(fields):
        return lax.all_to_all(fields, "ctx", 0, 0, axis_index_groups=shard_groups, tiled=True)

    if paired:
        (fields,) = rows_step(residual, onward=(0, input_gain, project_in), place=place)
    before, into = None, project_in
    for layer in range(LAYERS):
        out = project_out[layer]
        if paired:
            peer = lax.ppermute(residual, "head", swap)
            out, _ = lax.optimization_barrier((out, peer if before is None else before))
            weights_out = [out, lax.ppermute(out, "head", swap)]
            slots = rows_step(peer, (), (layer, input_gain, into), place, True, 20)
            received = [slots[0]]
            for slot in range(1, local_heads):
                partners = [(c, c ^ (replicas * slot)) for c in range(shards)]
                received.append(lax.ppermute(slots[slot], "ctx", partners))
            own = [to_heads(fields), assemble(received, place)]
            others = [lax.ppermute(chunk, "ctx", neighbours) for chunk in own]
            before = own[1]
        else:
            weights_out = [lax.all_gather(out, "head", axis=0, tiled=True)]
            gathered = lax.all_gather(residual, "head", axis=0, tiled=True)
            own = [to_heads(project(gathered, input_gain, project_in[layer], layer, place))]
            others = []
            if replicas > 1:
                others = [lax.all_gather(own[0], "ctx", axis=0, axis_index_groups=head_groups)]
                if replicas == 2:
                    others = [lax.ppermute(own[0], "ctx", neighbours)]
        heads = attention(layer, replicas, output_gain, own, others, first_place, place, split)
        if paired:
            into, _ = lax.optimization_barrier((project_in, heads))
            into = into[(layer + 1) % LAYERS]
        heads = heads.reshape(split * local_heads, HD, tokens // split)
        mixed = lax.all_to_all(heads, ("ctx", "head"), 0, 0, axis_index_groups=row_groups, tiled=True)
        mixed = (mixed.reshape(split * depth, tokens // split), layer, weights_out, weight_starts)
        if paired and layer + 1 < LAYERS:
            residual, fields = rows_step(residual, mixed, (layer + 1, input_gain, into), place)
        else:
            (residual,) = rows_step(residual, mixed)
    return residual


def solution(mesh):
    return jax.shard_map(
        per_device,
        mesh=mesh,
        in_specs=(
            P(("ctx", "head"), None),
            P(),
            P(None, None, None, "head"),
            P(None, "head"),
            P(None, "head", None),
        ),
        out_specs=P(("ctx", "head"), None),
        check_vma=False,
    )
```

```python
import functools

import jax
import jax.numpy as jnp
from jax import lax
from jax.experimental import pallas as pl
from jax.experimental.pallas import tpu as pltpu
from jax.sharding import PartitionSpec as P

HD = 64
LAYERS = 2
EPSILON = 1e-06
VMEM = pl.BlockSpec(memory_space=pltpu.VMEM)
HBM = pl.BlockSpec(memory_space=pltpu.HBM)


def params(mebibytes):
    return pltpu.CompilerParams(vmem_limit_bytes=mebibytes * 2**20)


def rms_scale(values, gain):
    mean_square = jnp.mean(values * values, axis=-1, keepdims=True)
    return values * lax.rsqrt(mean_square + EPSILON) * gain


def fetch(pairs, semaphores):
    copies = [pltpu.make_async_copy(*pair, semaphores.at[index]) for index, pair in enumerate(pairs)]
    for copy in copies:
        copy.start()
    return copies


def project_rows(rows, gain, weights, flat, place, outs):
    normed = rms_scale(rows, gain).astype(jnp.bfloat16)
    for which in range(3):
        field = jnp.dot(normed, weights(which), preferred_element_type=jnp.float32)
        flipped = field.T.astype(jnp.bfloat16)
        part = slice(which * HD, (which + 1) * HD)
        if len(outs) == 1:
            for head in range(outs[0].shape[0]):
                outs[0][head, part, :] = flipped[head * HD : (head + 1) * HD]
        else:
            flat[...] = flipped
            for slot, out in enumerate(outs):
                start = (place()[0] ^ slot) * HD
                out[part, :] = flat[pl.ds(pl.multiple_of(start, HD), HD), :]


def project(rows, gain, weights, layer, place):
    width, columns = weights.shape[1:]
    tokens = rows.shape[0]

    def kernel(row_ref, gain_ref, weight_ref, out_ref):
        values = row_ref[...].astype(jnp.float32)
        project_rows(values, gain_ref[layer : layer + 1, :], lambda which: weight_ref[which], None, place, [out_ref])

    return pl.pallas_call(
        kernel,
        in_specs=[VMEM] * 3,
        out_specs=VMEM,
        out_shape=jax.ShapeDtypeStruct((columns // HD, 3 * HD, tokens), jnp.bfloat16),
        compiler_params=params(16),
        cost_estimate=pl.CostEstimate(
            flops=6 * tokens * width * columns, bytes_accessed=6 * width * columns, transcendentals=0
        ),
    )(rows, gain, weights)


def mix_rows(starts, mixed, residual, weights):
    total = residual.astype(jnp.float32)
    for start, weight in zip(starts, weights):
        rows = weight.shape[0]
        at = start if isinstance(start, int) else pl.multiple_of(start, rows)
        total += jnp.dot(mixed[pl.ds(at, rows), :].T, weight[...], preferred_element_type=jnp.float32)
    return total.astype(jnp.bfloat16)


def rows_step(residual, mixed=(), onward=(), place=None, slots=False, weight=1, keep=False):
    rows, width = residual.shape
    operands, views, shapes, outs = [residual], [None], [(residual.shape, jnp.bfloat16)], []
    flops, itself = 0, False
    if mixed:
        entries, index, parts, starts = mixed
        operands += [entries] + list(parts)
        views += [None] + [index if len(part.shape) == 3 else None for part in parts]
        shapes += [(entries.shape, jnp.bfloat16)] + [(part.shape[-2:], jnp.bfloat16) for part in parts]
        outs.append((pltpu.VMEM if onward else jax.ShapeDtypeStruct)(residual.shape, jnp.bfloat16))
        flops += 2 * rows * width * entries.shape[0]
    if onward:
        layer, gain, project_in = onward
        columns = project_in.shape[-1]
        itself = len(project_in.shape) == 4
        operands += [gain] + [project_in] * (3 if itself else 1)
        views += [None] + [(layer, which) for which in range(3)]
        shapes += [(gain.shape, jnp.float32)] + [(project_in.shape[2:], jnp.bfloat16)] * (0 if keep else 3)
        shape, heads = (3 * HD, rows), columns // HD
        outs += [pltpu.VMEM(shape if slots else (heads, *shape), jnp.bfloat16)] * (heads if slots else 1)
        if keep:
            outs.append(pltpu.VMEM(project_in.shape[1:], jnp.bfloat16))
        flops += 6 * rows * width * columns
    count = len(operands)
    scratch = [pltpu.VMEM(*shape) for shape in shapes] + [pltpu.SemaphoreType.DMA((count,))] if itself else []
    if onward and slots:
        scratch.append(pltpu.VMEM((columns, rows), jnp.bfloat16))

    def kernel(*refs):
        sources, results, held = refs[:count], list(refs[count : count + len(outs)]), refs[count + len(outs) :]
        flat = refs[-1] if slots else None
        if keep:
            kept = results.pop()
            held = (*held[: count - 3], *(kept.at[which] for which in range(3)), *held[count - 3 :])
        if itself:
            pairs = [(ref if view is None else ref.at[view], to) for ref, view, to in zip(sources, views, held)]
            copies = fetch(pairs, held[count])
        else:
            held = sources

        def arrived(index):
            if itself:
                copies[index].wait()
            return held[index]

        current, used = arrived(0)[...], 1
        if mixed:
            used = 2 + len(parts)
            current = mix_rows(starts(), arrived(1), current, [arrived(index) for index in range(2, used)])
            results.pop(0)[...] = current
        if onward:
            scale = arrived(used)[layer : layer + 1, :]

            def weights(which):
                return arrived(used + 1 + which)[...] if itself else held[used + 1][which]

            project_rows(current.astype(jnp.float32), scale, weights, flat, place, results)

    if itself:
        operands = [pltpu.with_memory_space_constraint(operand, pltpu.HBM) for operand in operands]
    return pl.pallas_call(
        kernel,
        in_specs=[HBM if itself else VMEM] * count,
        out_specs=[VMEM] * len(outs),
        out_shape=outs,
        scratch_shapes=scratch,
        compiler_params=params(16),
        cost_estimate=pl.CostEstimate(flops=flops * weight, bytes_accessed=flops // rows, transcendentals=0),
    )(*operands)


def assemble(slots, place):
    def kernel(*refs):
        for slot, ref in enumerate(refs[:-1]):
            refs[-1][place()[0] ^ slot] = ref[...]

    return pl.pallas_call(
        kernel,
        in_specs=[VMEM] * len(slots),
        out_specs=VMEM,
        out_shape=pltpu.VMEM((len(slots), *slots[0].shape), slots[0].dtype),
        compiler_params=params(8),
        cost_estimate=pl.CostEstimate(flops=0, bytes_accessed=4 * len(slots) * slots[0].size, transcendentals=0),
    )(*slots)


def attention_kernel(layer, own_count, start, place, gain_ref, *refs):
    out_ref, keys, values = refs[-3:]
    own, others = refs[:own_count], refs[own_count:-3]
    groups, split, piece = out_ref.shape[1], out_ref.shape[0], out_ref.shape[-1]
    tokens = split * piece
    span = values.shape[1] // groups
    sources = span // tokens
    width = own[0].shape[-1]
    head, replica = place()

    def part(source, chunk, group, which):
        rows = slice(which * HD, (which + 1) * HD)
        if sources > 2:
            return others[0][source, group, rows, :]
        return (others if source else own)[chunk][group, rows, :]

    for group in range(groups):
        for source in range(sources):
            for chunk in range(own_count):
                first = group * span + source * tokens + chunk * width
                keys[first : first + width, :] = part(source, chunk, group, 1).T
                values[:, first : first + width] = part(source, chunk, group, 2)

    def shift(source):
        if sources == 2:
            return source * (2 * replica - 1)
        return replica - source

    def places(axis):
        place = lax.broadcasted_iota(jnp.int32, (tokens, tokens), axis) + start()
        return jnp.where(place >= tokens, place - tokens, place)

    ahead = places(0) - places(1)
    visible = [ahead <= shift(source) * tokens for source in range(sources)]
    gains = gain_ref[layer : layer + 1, :]
    gain = sum(
        jnp.where(head == index, gains[:, index * HD : (index + 1) * HD], 0.0) for index in range(gains.shape[1] // HD)
    ).T
    step = min(span, 512)
    for group in range(groups):
        query = jnp.concatenate([ref[group, :HD, :] for ref in own], axis=1)
        total = jnp.zeros((HD, tokens), jnp.float32)
        for first in range(0, (group + 1) * span, step):
            scores = jnp.dot(keys[first : first + step, :], query, preferred_element_type=jnp.float32)
            weights = scores * scores
            if first >= group * span:
                source = (first - group * span) // tokens
                mask = jnp.concatenate(visible[source : source + step // tokens], axis=0)
                weights = jnp.where(mask, weights, 0.0)
            total += jnp.dot(
                values[:, first : first + step], weights.astype(jnp.bfloat16), preferred_element_type=jnp.float32
            )
        mean_square = jnp.mean(total * total, axis=0, keepdims=True)
        scaled = (total * lax.rsqrt(mean_square + EPSILON) * gain).astype(jnp.bfloat16)
        for index in range(split):
            lanes = scaled[:, index * piece : (index + 1) * piece]
            if own_count == 1:
                out_ref[index, group] = lanes
            else:
                out_ref[start() // width if index == 0 else 1 - start() // width, group] = lanes


def attention(layer, sources, gain, own, others, start, place, split):
    groups = own[0].shape[0]
    tokens = sum(chunk.shape[2] for chunk in own)
    pairs = groups * (groups + 1) // 2 * sources * tokens * tokens

    def kernel(*refs):
        attention_kernel(layer, len(own), start, place, *refs)

    return pl.pallas_call(
        kernel,
        in_specs=[VMEM] * (1 + len(own) + len(others)),
        out_specs=VMEM,
        out_shape=jax.ShapeDtypeStruct((split, groups, HD, tokens // split), jnp.bfloat16),
        scratch_shapes=[
            pltpu.VMEM((groups * sources * tokens, HD), jnp.bfloat16),
            pltpu.VMEM((HD, groups * sources * tokens), jnp.bfloat16),
        ],
        compiler_params=params(16),
        cost_estimate=pl.CostEstimate(flops=4 * pairs * HD, bytes_accessed=2**21, transcendentals=0),
    )(gain, *own, *others)


def per_device(residual, input_gain, project_in, output_gain, project_out):
    shards, split = lax.axis_size("ctx"), lax.axis_size("head")
    depth = output_gain.shape[1]
    local_heads = depth // HD
    replicas = shards // local_heads
    paired = split == 2 and replicas == 2 and local_heads & (local_heads - 1) == 0
    swap = [(0, 1), (1, 0)]
    neighbours = [(c, c ^ 1) for c in range(shards)]
    rows = residual.shape[0]
    tokens = rows * split

    shard_groups = [[k * replicas + r for k in range(local_heads)] for r in range(replicas)]
    row_groups = [[c * split + x for x in range(split) for c in group] for group in shard_groups]
    head_groups = [[k * replicas + r for r in range(replicas)] for k in range(local_heads)]

    def weight_starts():
        if not paired:
            return [0]
        mine = lax.axis_index("head")
        return [mine * depth, (1 - mine) * depth]

    def place():
        index = lax.axis_index("ctx")
        return index // replicas, index % replicas

    def first_place():
        return lax.axis_index("head") * rows if paired else 0

    def to_heads(fields):
        return lax.all_to_all(fields, "ctx", 0, 0, axis_index_groups=shard_groups, tiled=True)

    if paired:
        fields, into = rows_step(residual, onward=(0, input_gain, project_in), place=place, keep=True)
    for layer in range(LAYERS):
        if paired:
            peer = lax.ppermute(residual, "head", swap)
            before = peer if layer == 0 else before
            out, _ = lax.optimization_barrier((project_out[layer], before))
            weights_out = [out, lax.ppermute(out, "head", swap)]
            slots = rows_step(peer, (), (layer, input_gain, into), place, True, 20)
            received = [slots[0]]
            for slot in range(1, local_heads):
                partners = [(c, c ^ (replicas * slot)) for c in range(shards)]
                received.append(lax.ppermute(slots[slot], "ctx", partners))
            own = [to_heads(fields), assemble(received, place)]
            before = own[1]
            others = [lax.ppermute(chunk, "ctx", neighbours) for chunk in own]
        else:
            weights_out = [lax.all_gather(project_out[layer], "head", axis=0, tiled=True)]
            gathered = lax.all_gather(residual, "head", axis=0, tiled=True)
            own = [to_heads(project(gathered, input_gain, project_in[layer], layer, place))]
            others = []
            if replicas > 1:
                others = [lax.all_gather(own[0], "ctx", axis=0, axis_index_groups=head_groups)]
                if replicas == 2:
                    others = [lax.ppermute(own[0], "ctx", neighbours)]
        heads = attention(layer, replicas, output_gain, own, others, first_place, place, split)
        if paired:
            into, _ = lax.optimization_barrier((project_in, heads))
            into = into[(layer + 1) % LAYERS]
        heads = heads.reshape(split * local_heads, HD, tokens // split)
        mixed = lax.all_to_all(heads, ("ctx", "head"), 0, 0, axis_index_groups=row_groups, tiled=True)
        mixed = (mixed.reshape(split * depth, tokens // split), layer, weights_out, weight_starts)
        if paired and layer + 1 < LAYERS:
            residual, fields = rows_step(residual, mixed, (layer + 1, input_gain, into), place)
        else:
            (residual,) = rows_step(residual, mixed)
    return residual


def solution(mesh):
    return jax.shard_map(
        per_device,
        mesh=mesh,
        in_specs=(
            P(("ctx", "head"), None),
            P(),
            P(None, None, None, "head"),
            P(None, "head"),
            P(None, "head", None),
        ),
        out_specs=P(("ctx", "head"), None),
        check_vma=False,
    )
```

```python
import functools

import jax
import jax.numpy as jnp
from jax import lax
from jax.experimental import pallas as pl
from jax.experimental.pallas import tpu as pltpu
from jax.sharding import PartitionSpec as P

HD = 64
LAYERS = 2
EPSILON = 1e-06
VMEM = pl.BlockSpec(memory_space=pltpu.VMEM)
HBM = pl.BlockSpec(memory_space=pltpu.HBM)


def params(mebibytes):
    return pltpu.CompilerParams(vmem_limit_bytes=mebibytes * 2**20)


def rms_scale(values, gain):
    mean_square = jnp.mean(values * values, axis=-1, keepdims=True)
    return values * lax.rsqrt(mean_square + EPSILON) * gain


def fetch(pairs, semaphores):
    copies = [pltpu.make_async_copy(*pair, semaphores.at[index]) for index, pair in enumerate(pairs)]
    for copy in copies:
        copy.start()
    return copies


def project_rows(rows, gain, weights, flat, place, outs):
    normed = rms_scale(rows, gain).astype(jnp.bfloat16)
    for which in range(3):
        field = jnp.dot(normed, weights(which), preferred_element_type=jnp.float32)
        flipped = field.T.astype(jnp.bfloat16)
        part = slice(which * HD, (which + 1) * HD)
        if len(outs) == 1:
            for head in range(outs[0].shape[0]):
                outs[0][head, part, :] = flipped[head * HD : (head + 1) * HD]
        else:
            flat[...] = flipped
            for slot, out in enumerate(outs):
                start = (place()[0] ^ slot) * HD
                out[part, :] = flat[pl.ds(pl.multiple_of(start, HD), HD), :]


def project(rows, gain, weights, layer, place):
    width, columns = weights.shape[1:]
    tokens = rows.shape[0]

    def kernel(row_ref, gain_ref, weight_ref, out_ref):
        values = row_ref[...].astype(jnp.float32)
        project_rows(values, gain_ref[layer : layer + 1, :], lambda which: weight_ref[which], None, place, [out_ref])

    return pl.pallas_call(
        kernel,
        in_specs=[VMEM] * 3,
        out_specs=VMEM,
        out_shape=jax.ShapeDtypeStruct((columns // HD, 3 * HD, tokens), jnp.bfloat16),
        compiler_params=params(16),
        cost_estimate=pl.CostEstimate(
            flops=6 * tokens * width * columns, bytes_accessed=6 * width * columns, transcendentals=0
        ),
    )(rows, gain, weights)


def mix_rows(starts, mixed, residual, weights):
    total = residual.astype(jnp.float32)
    for start, weight in zip(starts, weights):
        rows = weight.shape[0]
        at = start if isinstance(start, int) else pl.multiple_of(start, rows)
        total += jnp.dot(mixed[pl.ds(at, rows), :].T, weight[...], preferred_element_type=jnp.float32)
    return total.astype(jnp.bfloat16)


def rows_step(residual, mixed=(), onward=(), place=None, slots=False, weight=1, keep=False):
    rows, width = residual.shape
    operands, views, shapes, outs = [residual], [None], [(residual.shape, jnp.bfloat16)], []
    flops, itself = 0, False
    if mixed:
        entries, index, parts, starts = mixed
        operands += [entries] + list(parts)
        views += [None] + [index if len(part.shape) == 3 else None for part in parts]
        shapes += [(entries.shape, jnp.bfloat16)] + [(part.shape[-2:], jnp.bfloat16) for part in parts]
        outs.append((pltpu.VMEM if onward else jax.ShapeDtypeStruct)(residual.shape, jnp.bfloat16))
        flops += 2 * rows * width * entries.shape[0]
    if onward:
        layer, gain, project_in = onward
        columns = project_in.shape[-1]
        itself = len(project_in.shape) == 4
        operands += [gain] + [project_in] * (3 if itself else 1)
        views += [None] + [(layer, which) for which in range(3)]
        shapes += [(gain.shape, jnp.float32)] + [(project_in.shape[2:], jnp.bfloat16)] * (0 if keep else 3)
        shape, heads = (3 * HD, rows), columns // HD
        outs += [pltpu.VMEM(shape if slots else (heads, *shape), jnp.bfloat16)] * (heads if slots else 1)
        if keep:
            outs.append(pltpu.VMEM(project_in.shape[1:], jnp.bfloat16))
        flops += 6 * rows * width * columns
    count = len(operands)
    scratch = [pltpu.VMEM(*shape) for shape in shapes] + [pltpu.SemaphoreType.DMA((count,))] if itself else []
    if onward and slots:
        scratch.append(pltpu.VMEM((columns, rows), jnp.bfloat16))

    def kernel(*refs):
        sources, results, held = refs[:count], list(refs[count : count + len(outs)]), refs[count + len(outs) :]
        flat = refs[-1] if slots else None
        if keep:
            kept = results.pop()
            held = (*held[: count - 3], *(kept.at[which] for which in range(3)), *held[count - 3 :])
        if itself:
            pairs = [(ref if view is None else ref.at[view], to) for ref, view, to in zip(sources, views, held)]
            copies = fetch(pairs, held[count])
        else:
            held = sources

        def arrived(index):
            if itself:
                copies[index].wait()
            return held[index]

        current, used = arrived(0)[...], 1
        if mixed:
            used = 2 + len(parts)
            current = mix_rows(starts(), arrived(1), current, [arrived(index) for index in range(2, used)])
            results.pop(0)[...] = current
        if onward:
            scale = arrived(used)[layer : layer + 1, :]

            def weights(which):
                return arrived(used + 1 + which)[...] if itself else held[used + 1][which]

            project_rows(current.astype(jnp.float32), scale, weights, flat, place, results)

    if itself:
        operands = [pltpu.with_memory_space_constraint(operand, pltpu.HBM) for operand in operands]
    return pl.pallas_call(
        kernel,
        in_specs=[HBM if itself else VMEM] * count,
        out_specs=[VMEM] * len(outs),
        out_shape=outs,
        scratch_shapes=scratch,
        compiler_params=params(16),
        cost_estimate=pl.CostEstimate(flops=flops * weight, bytes_accessed=flops // rows, transcendentals=0),
    )(*operands)


def slot_order(count):
    return [*range(count // 2), *range(count - 1, count // 2 - 1, -1)]


def assemble(slots, place):
    order = slot_order(len(slots))

    def kernel(*refs):
        for slot, ref in zip(order, refs):
            refs[-1][place()[0] ^ slot] = ref[...]

    return pl.pallas_call(
        kernel,
        in_specs=[VMEM] * len(slots),
        out_specs=VMEM,
        out_shape=pltpu.VMEM((len(slots), *slots[0].shape), slots[0].dtype),
        compiler_params=params(8),
        cost_estimate=pl.CostEstimate(flops=0, bytes_accessed=4 * len(slots) * slots[0].size, transcendentals=0),
    )(*(slots[slot] for slot in order))


def attention_kernel(layer, own_count, start, place, gain_ref, *refs):
    out_ref, keys, values = refs[-3:]
    own, others = refs[:own_count], refs[own_count:-3]
    groups, split, piece = out_ref.shape[1], out_ref.shape[0], out_ref.shape[-1]
    tokens = split * piece
    span = values.shape[1] // groups
    sources = span // tokens
    width = own[0].shape[-1]
    head, replica = place()

    def part(source, chunk, group, which):
        rows = slice(which * HD, (which + 1) * HD)
        if sources > 2:
            return others[0][source, group, rows, :]
        return (others if source else own)[chunk][group, rows, :]

    for group in range(groups):
        for source in range(sources):
            for chunk in range(own_count):
                first = group * span + source * tokens + chunk * width
                keys[first : first + width, :] = part(source, chunk, group, 1).T
                values[:, first : first + width] = part(source, chunk, group, 2)

    def shift(source):
        if sources == 2:
            return source * (2 * replica - 1)
        return replica - source

    def places(axis):
        place = lax.broadcasted_iota(jnp.int32, (tokens, tokens), axis) + start()
        return jnp.where(place >= tokens, place - tokens, place)

    ahead = places(0) - places(1)
    visible = [ahead <= shift(source) * tokens for source in range(sources)]
    gains = gain_ref[layer : layer + 1, :]
    gain = sum(
        jnp.where(head == index, gains[:, index * HD : (index + 1) * HD], 0.0) for index in range(gains.shape[1] // HD)
    ).T
    step = min(span, 512)
    for group in range(groups):
        query = jnp.concatenate([ref[group, :HD, :] for ref in own], axis=1)
        total = jnp.zeros((HD, tokens), jnp.float32)
        for first in range(0, (group + 1) * span, step):
            scores = jnp.dot(keys[first : first + step, :], query, preferred_element_type=jnp.float32)
            weights = scores * scores
            if first >= group * span:
                source = (first - group * span) // tokens
                mask = jnp.concatenate(visible[source : source + step // tokens], axis=0)
                weights = jnp.where(mask, weights, 0.0)
            total += jnp.dot(
                values[:, first : first + step], weights.astype(jnp.bfloat16), preferred_element_type=jnp.float32
            )
        mean_square = jnp.mean(total * total, axis=0, keepdims=True)
        scaled = (total * lax.rsqrt(mean_square + EPSILON) * gain).astype(jnp.bfloat16)
        for index in range(split):
            lanes = scaled[:, index * piece : (index + 1) * piece]
            if own_count == 1:
                out_ref[index, group] = lanes
            else:
                out_ref[start() // width if index == 0 else 1 - start() // width, group] = lanes


def attention(layer, sources, gain, own, others, start, place, split):
    groups = own[0].shape[0]
    tokens = sum(chunk.shape[2] for chunk in own)
    pairs = groups * (groups + 1) // 2 * sources * tokens * tokens

    def kernel(*refs):
        attention_kernel(layer, len(own), start, place, *refs)

    return pl.pallas_call(
        kernel,
        in_specs=[VMEM] * (1 + len(own) + len(others)),
        out_specs=VMEM,
        out_shape=jax.ShapeDtypeStruct((split, groups, HD, tokens // split), jnp.bfloat16),
        scratch_shapes=[
            pltpu.VMEM((groups * sources * tokens, HD), jnp.bfloat16),
            pltpu.VMEM((HD, groups * sources * tokens), jnp.bfloat16),
        ],
        compiler_params=params(16),
        cost_estimate=pl.CostEstimate(flops=4 * pairs * HD, bytes_accessed=2**21, transcendentals=0),
    )(gain, *own, *others)


def per_device(residual, input_gain, project_in, output_gain, project_out):
    shards, split = lax.axis_size("ctx"), lax.axis_size("head")
    depth = output_gain.shape[1]
    local_heads = depth // HD
    replicas = shards // local_heads
    paired = split == 2 and replicas == 2 and local_heads & (local_heads - 1) == 0
    swap = [(0, 1), (1, 0)]
    neighbours = [(c, c ^ 1) for c in range(shards)]
    rows = residual.shape[0]
    tokens = rows * split

    shard_groups = [[k * replicas + r for k in range(local_heads)] for r in range(replicas)]
    row_groups = [[c * split + x for x in range(split) for c in group] for group in shard_groups]
    head_groups = [[k * replicas + r for r in range(replicas)] for k in range(local_heads)]

    def weight_starts():
        if not paired:
            return [0]
        mine = lax.axis_index("head")
        return [mine * depth, (1 - mine) * depth]

    def place():
        index = lax.axis_index("ctx")
        return index // replicas, index % replicas

    def first_place():
        return lax.axis_index("head") * rows if paired else 0

    def to_heads(fields):
        return lax.all_to_all(fields, "ctx", 0, 0, axis_index_groups=shard_groups, tiled=True)

    if paired:
        fields, into = rows_step(residual, onward=(0, input_gain, project_in), place=place, keep=True)
    for layer in range(LAYERS):
        if paired:
            peer = lax.ppermute(residual, "head", swap)
            if layer == 0:
                out, _ = lax.optimization_barrier((project_out, peer))
                out = out[0]
            weights_out = [out, lax.ppermute(out, "head", swap)]
            slots = rows_step(peer, (), (layer, input_gain, into), place, True, 20)
            received = list(slots)
            for slot in slot_order(local_heads)[1:]:
                partners = [(c, c ^ (replicas * slot)) for c in range(shards)]
                received[slot] = lax.ppermute(slots[slot], "ctx", partners)
            own = [to_heads(fields), assemble(received, place)]
            others = [lax.ppermute(chunk, "ctx", neighbours) for chunk in own]
        else:
            weights_out = [lax.all_gather(project_out[layer], "head", axis=0, tiled=True)]
            gathered = lax.all_gather(residual, "head", axis=0, tiled=True)
            own = [to_heads(project(gathered, input_gain, project_in[layer], layer, place))]
            others = []
            if replicas > 1:
                others = [lax.all_gather(own[0], "ctx", axis=0, axis_index_groups=head_groups)]
                if replicas == 2:
                    others = [lax.ppermute(own[0], "ctx", neighbours)]
        heads = attention(layer, replicas, output_gain, own, others, first_place, place, split)
        if paired:
            into, out, _ = lax.optimization_barrier((project_in, project_out, heads))
            into, out = into[(layer + 1) % LAYERS], out[(layer + 1) % LAYERS]
        heads = heads.reshape(split * local_heads, HD, tokens // split)
        mixed = lax.all_to_all(heads, ("ctx", "head"), 0, 0, axis_index_groups=row_groups, tiled=True)
        mixed = (mixed.reshape(split * depth, tokens // split), layer, weights_out, weight_starts)
        if paired and layer + 1 < LAYERS:
            residual, fields = rows_step(residual, mixed, (layer + 1, input_gain, into), place)
        else:
            (residual,) = rows_step(residual, mixed)
    return residual


def solution(mesh):
    return jax.shard_map(
        per_device,
        mesh=mesh,
        in_specs=(
            P(("ctx", "head"), None),
            P(),
            P(None, None, None, "head"),
            P(None, "head"),
            P(None, "head", None),
        ),
        out_specs=P(("ctx", "head"), None),
        check_vma=False,
    )
```

```python
import functools

import jax
import jax.numpy as jnp
from jax import lax
from jax.experimental import pallas as pl
from jax.experimental.pallas import tpu as pltpu
from jax.sharding import PartitionSpec as P

HD = 64
LAYERS = 2
EPSILON = 1e-06
VMEM = pl.BlockSpec(memory_space=pltpu.VMEM)
HBM = pl.BlockSpec(memory_space=pltpu.HBM)


def params(mebibytes):
    return pltpu.CompilerParams(vmem_limit_bytes=mebibytes * 2**20)


def rms_scale(values, gain):
    mean_square = jnp.mean(values * values, axis=-1, keepdims=True)
    return values * lax.rsqrt(mean_square + EPSILON) * gain


def fetch(pairs, semaphores):
    copies = [pltpu.make_async_copy(*pair, semaphores.at[index]) for index, pair in enumerate(pairs)]
    for copy in copies:
        copy.start()
    return copies


def project_rows(rows, gain, weights, flat, place, outs):
    normed = rms_scale(rows, gain).astype(jnp.bfloat16)
    for which in range(3):
        field = jnp.dot(normed, weights(which), preferred_element_type=jnp.float32)
        flipped = field.T.astype(jnp.bfloat16)
        part = slice(which * HD, (which + 1) * HD)
        if len(outs) == 1:
            for head in range(outs[0].shape[0]):
                outs[0][head, part, :] = flipped[head * HD : (head + 1) * HD]
        else:
            flat[...] = flipped
            for slot, out in enumerate(outs):
                start = (place()[0] ^ slot) * HD
                out[part, :] = flat[pl.ds(pl.multiple_of(start, HD), HD), :]


def project(rows, gain, weights, layer, place):
    width, columns = weights.shape[1:]
    tokens = rows.shape[0]

    def kernel(row_ref, gain_ref, weight_ref, out_ref):
        values = row_ref[...].astype(jnp.float32)
        project_rows(values, gain_ref[layer : layer + 1, :], lambda which: weight_ref[which], None, place, [out_ref])

    return pl.pallas_call(
        kernel,
        in_specs=[VMEM] * 3,
        out_specs=VMEM,
        out_shape=jax.ShapeDtypeStruct((columns // HD, 3 * HD, tokens), jnp.bfloat16),
        compiler_params=params(16),
        cost_estimate=pl.CostEstimate(
            flops=6 * tokens * width * columns, bytes_accessed=6 * width * columns, transcendentals=0
        ),
    )(rows, gain, weights)


def mix_rows(starts, mixed, residual, weights):
    total = residual.astype(jnp.float32)
    for start, weight in zip(starts, weights):
        rows = weight.shape[0]
        at = start if isinstance(start, int) else pl.multiple_of(start, rows)
        total += jnp.dot(mixed[pl.ds(at, rows), :].T, weight[...], preferred_element_type=jnp.float32)
    return total.astype(jnp.bfloat16)


def rows_step(residual, mixed=(), onward=(), place=None, slots=False, weight=1, keep=False):
    rows, width = residual.shape
    operands, views, shapes, outs = [residual], [None], [(residual.shape, jnp.bfloat16)], []
    flops, itself = 0, False
    if mixed:
        entries, index, parts, starts = mixed
        operands += [entries] + list(parts)
        views += [None] + [index if len(part.shape) == 3 else None for part in parts]
        shapes += [(entries.shape, jnp.bfloat16)] + [(part.shape[-2:], jnp.bfloat16) for part in parts]
        outs.append((pltpu.VMEM if onward else jax.ShapeDtypeStruct)(residual.shape, jnp.bfloat16))
        flops += 2 * rows * width * entries.shape[0]
    if onward:
        layer, gain, project_in = onward
        columns = project_in.shape[-1]
        itself = len(project_in.shape) == 4
        operands += [gain] + [project_in] * (3 if itself else 1)
        views += [None] + [(layer, which) for which in range(3)]
        shapes += [(gain.shape, jnp.float32)] + [(project_in.shape[2:], jnp.bfloat16)] * (0 if keep else 3)
        shape, heads = (3 * HD, rows), columns // HD
        outs += [pltpu.VMEM(shape, jnp.bfloat16)] * heads if slots else [pltpu.HBM((heads, *shape), jnp.bfloat16)]
        if keep:
            outs.append(pltpu.VMEM(project_in.shape[1:], jnp.bfloat16))
        flops += 6 * rows * width * columns
    count = len(operands)
    scratch = [pltpu.VMEM(*shape) for shape in shapes] + [pltpu.SemaphoreType.DMA((count,))] if itself else []
    if onward and slots:
        scratch.append(pltpu.VMEM((columns, rows), jnp.bfloat16))

    def kernel(*refs):
        sources, results, held = refs[:count], list(refs[count : count + len(outs)]), refs[count + len(outs) :]
        flat = refs[-1] if slots else None
        if keep:
            kept = results.pop()
            held = (*held[: count - 3], *(kept.at[which] for which in range(3)), *held[count - 3 :])
        if itself:
            pairs = [(ref if view is None else ref.at[view], to) for ref, view, to in zip(sources, views, held)]
            copies = fetch(pairs, held[count])
        else:
            held = sources

        def arrived(index):
            if itself:
                copies[index].wait()
            return held[index]

        current, used = arrived(0)[...], 1
        if mixed:
            used = 2 + len(parts)
            current = mix_rows(starts(), arrived(1), current, [arrived(index) for index in range(2, used)])
            results.pop(0)[...] = current
        if onward:
            scale = arrived(used)[layer : layer + 1, :]

            def weights(which):
                return arrived(used + 1 + which)[...] if itself else held[used + 1][which]

            project_rows(current.astype(jnp.float32), scale, weights, flat, place, results)

    if itself:
        operands = [pltpu.with_memory_space_constraint(operand, pltpu.HBM) for operand in operands]
    return pl.pallas_call(
        kernel,
        in_specs=[HBM if itself else VMEM] * count,
        out_specs=[VMEM] * len(outs),
        out_shape=outs,
        scratch_shapes=scratch,
        compiler_params=params(16),
        cost_estimate=pl.CostEstimate(flops=flops * weight, bytes_accessed=flops // rows, transcendentals=0),
    )(*operands)


def slot_order(count):
    half = count // 2
    return [0, *range(half - 1, 0, -1), *range(count - 1, half - 1, -1)]


def assemble(slots, place):
    order = slot_order(len(slots))

    def kernel(*refs):
        for slot, ref in zip(order, refs):
            refs[-1][place()[0] ^ slot] = ref[...]

    return pl.pallas_call(
        kernel,
        in_specs=[VMEM] * len(slots),
        out_specs=VMEM,
        out_shape=pltpu.VMEM((len(slots), *slots[0].shape), slots[0].dtype),
        compiler_params=params(8),
        cost_estimate=pl.CostEstimate(flops=0, bytes_accessed=4 * len(slots) * slots[0].size, transcendentals=0),
    )(*(slots[slot] for slot in order))


def attention_kernel(layer, own_count, start, place, gain_ref, *refs):
    out_ref, keys, values = refs[-3:]
    own, others = refs[:own_count], refs[own_count:-3]
    groups, split, piece = out_ref.shape[1], out_ref.shape[0], out_ref.shape[-1]
    tokens = split * piece
    span = values.shape[1] // groups
    sources = span // tokens
    width = own[0].shape[-1]
    head, replica = place()

    def part(source, chunk, group, which):
        rows = slice(which * HD, (which + 1) * HD)
        if sources > 2:
            return others[0][source, group, rows, :]
        return (others if source else own)[chunk][group, rows, :]

    for group in range(groups):
        for source in range(sources):
            for chunk in range(own_count):
                first = group * span + source * tokens + chunk * width
                keys[first : first + width, :] = part(source, chunk, group, 1).T
                values[:, first : first + width] = part(source, chunk, group, 2)

    def shift(source):
        if sources == 2:
            return source * (2 * replica - 1)
        return replica - source

    def places(axis):
        place = lax.broadcasted_iota(jnp.int32, (tokens, tokens), axis) + start()
        return jnp.where(place >= tokens, place - tokens, place)

    ahead = places(0) - places(1)
    visible = [ahead <= shift(source) * tokens for source in range(sources)]
    gains = gain_ref[layer : layer + 1, :]
    gain = sum(
        jnp.where(head == index, gains[:, index * HD : (index + 1) * HD], 0.0) for index in range(gains.shape[1] // HD)
    ).T
    step = min(span, 512)
    for group in range(groups):
        query = jnp.concatenate([ref[group, :HD, :] for ref in own], axis=1)
        total = jnp.zeros((HD, tokens), jnp.float32)
        for first in range(0, (group + 1) * span, step):
            scores = jnp.dot(keys[first : first + step, :], query, preferred_element_type=jnp.float32)
            weights = scores * scores
            if first >= group * span:
                source = (first - group * span) // tokens
                mask = jnp.concatenate(visible[source : source + step // tokens], axis=0)
                weights = jnp.where(mask, weights, 0.0)
            total += jnp.dot(
                values[:, first : first + step], weights.astype(jnp.bfloat16), preferred_element_type=jnp.float32
            )
        mean_square = jnp.mean(total * total, axis=0, keepdims=True)
        scaled = (total * lax.rsqrt(mean_square + EPSILON) * gain).astype(jnp.bfloat16)
        for index in range(split):
            lanes = scaled[:, index * piece : (index + 1) * piece]
            if own_count == 1:
                out_ref[index, group] = lanes
            else:
                out_ref[start() // width if index == 0 else 1 - start() // width, group] = lanes


def attention(layer, sources, gain, own, others, start, place, split):
    groups = own[0].shape[0]
    tokens = sum(chunk.shape[2] for chunk in own)
    pairs = groups * (groups + 1) // 2 * sources * tokens * tokens

    def kernel(*refs):
        attention_kernel(layer, len(own), start, place, *refs)

    return pl.pallas_call(
        kernel,
        in_specs=[VMEM] * (1 + len(own) + len(others)),
        out_specs=VMEM,
        out_shape=jax.ShapeDtypeStruct((split, groups, HD, tokens // split), jnp.bfloat16),
        scratch_shapes=[
            pltpu.VMEM((groups * sources * tokens, HD), jnp.bfloat16),
            pltpu.VMEM((HD, groups * sources * tokens), jnp.bfloat16),
        ],
        compiler_params=params(16),
        cost_estimate=pl.CostEstimate(flops=4 * pairs * HD, bytes_accessed=2**21, transcendentals=0),
    )(gain, *own, *others)


def per_device(residual, input_gain, project_in, output_gain, project_out):
    shards, split = lax.axis_size("ctx"), lax.axis_size("head")
    depth = output_gain.shape[1]
    local_heads = depth // HD
    replicas = shards // local_heads
    paired = split == 2 and replicas == 2 and local_heads & (local_heads - 1) == 0
    swap = [(0, 1), (1, 0)]
    neighbours = [(c, c ^ 1) for c in range(shards)]
    rows = residual.shape[0]
    tokens = rows * split

    shard_groups = [[k * replicas + r for k in range(local_heads)] for r in range(replicas)]
    row_groups = [[c * split + x for x in range(split) for c in group] for group in shard_groups]
    head_groups = [[k * replicas + r for r in range(replicas)] for k in range(local_heads)]

    def weight_starts():
        if not paired:
            return [0]
        mine = lax.axis_index("head")
        return [mine * depth, (1 - mine) * depth]

    def place():
        index = lax.axis_index("ctx")
        return index // replicas, index % replicas

    def first_place():
        return lax.axis_index("head") * rows if paired else 0

    def to_heads(fields):
        return lax.all_to_all(fields, "ctx", 0, 0, axis_index_groups=shard_groups, tiled=True)

    if paired:
        fields, into = rows_step(residual, onward=(0, input_gain, project_in), place=place, keep=True)
    for layer in range(LAYERS):
        if paired:
            peer = lax.ppermute(residual, "head", swap)
            if layer == 0:
                out, _ = lax.optimization_barrier((project_out, peer))
                out = out[0]
            weights_out = [out, lax.ppermute(out, "head", swap)]
            slots = rows_step(peer, (), (layer, input_gain, into), place, True, 20)
            received = list(slots)
            for slot in slot_order(local_heads)[1:]:
                partners = [(c, c ^ (replicas * slot)) for c in range(shards)]
                received[slot] = lax.ppermute(slots[slot], "ctx", partners)
            own = [to_heads(fields), assemble(received, place)]
            others = [lax.ppermute(chunk, "ctx", neighbours) for chunk in own]
        else:
            weights_out = [lax.all_gather(project_out[layer], "head", axis=0, tiled=True)]
            gathered = lax.all_gather(residual, "head", axis=0, tiled=True)
            own = [to_heads(project(gathered, input_gain, project_in[layer], layer, place))]
            others = []
            if replicas > 1:
                others = [lax.all_gather(own[0], "ctx", axis=0, axis_index_groups=head_groups)]
                if replicas == 2:
                    others = [lax.ppermute(own[0], "ctx", neighbours)]
        heads = attention(layer, replicas, output_gain, own, others, first_place, place, split)
        if paired:
            into, out, _ = lax.optimization_barrier((project_in, project_out, heads))
            into, out = into[(layer + 1) % LAYERS], out[(layer + 1) % LAYERS]
        heads = heads.reshape(split * local_heads, HD, tokens // split)
        mixed = lax.all_to_all(heads, ("ctx", "head"), 0, 0, axis_index_groups=row_groups, tiled=True)
        mixed = (mixed.reshape(split * depth, tokens // split), layer, weights_out, weight_starts)
        if paired and layer + 1 < LAYERS:
            residual, fields = rows_step(residual, mixed, (layer + 1, input_gain, into), place)
        else:
            (residual,) = rows_step(residual, mixed)
    return residual


def solution(mesh):
    return jax.shard_map(
        per_device,
        mesh=mesh,
        in_specs=(
            P(("ctx", "head"), None),
            P(),
            P(None, None, None, "head"),
            P(None, "head"),
            P(None, "head", None),
        ),
        out_specs=P(("ctx", "head"), None),
        check_vma=False,
    )
```
